256 devices in a mesh: dp: 2 (over z_hi), context: 32 (over y, x, core), tensor: 4 (over z_lo).
Axes of the slice: x: 4, y: 4, z: 8 (z_hi: 2, z_lo: 4; z = z_hi * 4 + z_lo), core: 2. Of those that a mesh axis runs over, the one named last changes fastest.
Arguments:
- value_in: bfloat16 [2, 16384, 2048], P('dp', 'context', 'tensor'), may hold values from -7 to 7
- key_in: bfloat16 [2, 16384, 2048], P('dp', 'context', 'tensor'), may hold values from -7 to 7
- query_in: bfloat16 [2, 16384, 2048], P('dp', 'context', 'tensor'), may hold values from -7 to 7
- filter_taps: bfloat16 [16384, 2048], P('context', 'tensor'), may hold values from -8 to 8
- out_weight: bfloat16 [2048, 2048], P('tensor'), may hold values from -0.125 to 0.125
- cotangent: bfloat16 [2, 16384, 2048], P('dp', 'context', 'tensor'), may hold values from -7 to 7
Outputs:
- mixed_out: bfloat16 [2, 16384, 2048], P('dp', 'context', 'tensor')
- grad_value: bfloat16 [2, 16384, 2048], P('dp', 'context', 'tensor')
- grad_key: bfloat16 [2, 16384, 2048], P('dp', 'context', 'tensor')
- grad_query: bfloat16 [2, 16384, 2048], P('dp', 'context', 'tensor')
- grad_filter: float32 [16384, 2048], P('context', 'tensor')
The draws below stay inside these ranges and needn't reach their ends.
All inputs are finite; a program needn't handle non-finite values.
Results may differ from the reference program's by a relative error of at most 0.015.
Values may be sent and summed in bfloat16 or wider, within the bound.
No kernel may reach another device: no remote copies, remote signals or barrier semaphores. Data moves between devices by JAX's collectives and lax.ppermute only.
A program may use at most 128 MiB of HBM per device.

```python
import math
import jax
import jax.numpy as jnp
from jax import lax

CH = 2048
BLOCK = 512
SEQ = 2
LENGTH = 16384
RADIX = 64
POINTS = 32768


def channel_marks(key):
    picked = jax.random.randint(jax.random.fold_in(key, 101), (CH,), 0, 2).astype(jnp.float32)
    signed = (2 * jax.random.randint(jax.random.fold_in(key, 103), (CH,), 0, 2) - 1).astype(jnp.float32)
    return (picked, signed)


def draw_value_in(key, part):
    picked, signed = channel_marks(key)
    key = jax.random.fold_in(key, 31)
    noise = jnp.clip(jax.random.normal(key, (SEQ, LENGTH, CH), jnp.float32), -6.0, 6.0)
    return (noise + 0.7 * picked[None, None, :]).astype(jnp.bfloat16)


def draw_key_in(key, part):
    picked, signed = channel_marks(key)
    key = jax.random.fold_in(key, 37)
    noise = jnp.clip(jax.random.normal(key, (SEQ, LENGTH, CH), jnp.float32), -6.0, 6.0)
    return (noise + 0.7 * (picked * signed)[None, None, :]).astype(jnp.bfloat16)


def draw_query_in(key, part):
    picked, signed = channel_marks(key)
    key = jax.random.fold_in(key, 41)
    noise = jnp.clip(jax.random.normal(key, (SEQ, LENGTH, CH), jnp.float32), -6.0, 6.0)
    return (noise + 0.7 * (1.0 - picked)[None, None, :]).astype(jnp.bfloat16)


def draw_cotangent(key, part):
    picked, signed = channel_marks(key)
    key = jax.random.fold_in(key, 43)
    noise = jnp.clip(jax.random.normal(key, (SEQ, LENGTH, CH), jnp.float32), -6.0, 6.0)
    return (noise + 0.7 * ((1.0 - picked) * signed)[None, None, :]).astype(jnp.bfloat16)


def decaying(noise, rates, position):
    envelope = jnp.exp(-position * rates[None, :])
    level = jnp.sqrt(2.0 * rates / (LENGTH * (1.0 - jnp.exp(-2.0 * rates))))
    return noise * envelope * level[None, :]


def draw_filter_taps(key, part):
    key = jax.random.fold_in(key, 7)
    fast_rates = jnp.exp(jax.random.uniform(jax.random.fold_in(key, 11), (CH,), jnp.float32, math.log(0.1), math.log(300.0)))
    slow_rates = jnp.exp(jax.random.uniform(jax.random.fold_in(key, 29), (CH,), jnp.float32, math.log(0.3), math.log(3.0)))
    fraction = jnp.exp(jax.random.uniform(jax.random.fold_in(key, 43), (CH,), jnp.float32, math.log(1e-06), math.log(0.003)))
    shelf_sign = (2 * jax.random.randint(jax.random.fold_in(key, 47), (CH,), 0, 2) - 1).astype(jnp.float32)
    gain = jnp.exp(jax.random.uniform(jax.random.fold_in(key, 53), (CH,), jnp.float32, math.log(0.5), math.log(1.5)))
    head_key = jax.random.fold_in(key, 23)
    slow_key = jax.random.fold_in(key, 37)
    share_key = jax.random.fold_in(key, 41)
    head_noise = jnp.clip(jax.random.normal(head_key, (LENGTH, CH), jnp.float32), -6.0, 6.0)
    slow_noise = jnp.clip(jax.random.normal(slow_key, (LENGTH, CH), jnp.float32), -6.0, 6.0)
    share = jax.random.uniform(share_key, (CH,), jnp.float32, 0.05, 0.3)
    position = jnp.arange(LENGTH, dtype=jnp.float32)[:, None] / LENGTH
    head = decaying(head_noise, fast_rates, position)
    slow = decaying(slow_noise, slow_rates, position)
    start = LENGTH // 8
    beyond = (jnp.arange(LENGTH, dtype=jnp.int32) >= start).astype(jnp.float32)[:, None]
    shelf = beyond * (jnp.sqrt(fraction / (LENGTH - start)) * shelf_sign)[None, :]
    taps = gain[None, :] * (jnp.sqrt(1.0 - share)[None, :] * head + jnp.sqrt(share)[None, :] * slow + shelf)
    return jnp.clip(taps, -8.0, 8.0).astype(jnp.bfloat16)


def levels(stream_key, shape, pieces, least, largest):
    def one(dim, shards_of):
        heights = jax.random.uniform(jax.random.fold_in(jax.random.fold_in(stream_key, 6), dim), (shards_of,), jnp.float32, least / len(pieces), largest / len(pieces))
        return jnp.repeat(jnp.exp(heights), shape[dim] // shards_of).reshape((-1,) + (1,) * (len(shape) - dim - 1))

    level = one(*pieces[0])
    for cut in pieces[1:]:
        level = level * one(*cut)
    return level


def bell_draw(stream_key, extent, deviation, limit, pieces=(), held_as=jnp.bfloat16):
    array = deviation * jax.random.normal(stream_key, extent, jnp.float32)
    if pieces:
        array = array * levels(stream_key, extent, pieces, -0.22, 0.18)
    return jnp.clip(array, -limit, limit).astype(held_as)


def setup_inputs(seed: int = 0) -> dict:
    keys = jax.random.split(jax.random.key(seed), 7)
    return {
        "value_in": draw_value_in(jax.random.fold_in(keys[6], 71), 0),
        "key_in": draw_key_in(jax.random.fold_in(keys[6], 71), 0),
        "query_in": draw_query_in(jax.random.fold_in(keys[6], 71), 0),
        "filter_taps": draw_filter_taps(jax.random.fold_in(keys[6], 71), 0),
        "out_weight": bell_draw(keys[4], (CH, CH), CH ** -0.5, 0.125, ((0, 4),)),
        "cotangent": draw_cotangent(jax.random.fold_in(keys[6], 71), 0),
    }


def unit_wave(first_index, second_index, period):
    phase_angle = (first_index * second_index % period).astype(jnp.float32) * (-2.0 * math.pi / period)
    return (jnp.cos(phase_angle), jnp.sin(phase_angle))

def spectral_tables(row_count, block_size):
    radix_size = 2 * row_count
    radix_cos, radix_sin = unit_wave(jnp.arange(row_count, dtype=jnp.int32)[:, None], jnp.arange(radix_size, dtype=jnp.int32)[None, :], radix_size)
    radix_cos = radix_cos.astype(jnp.bfloat16)
    radix_sin = radix_sin.astype(jnp.bfloat16)
    radix_fwd = jnp.stack([radix_cos, radix_sin], 0)
    radix_inv = jnp.stack([radix_cos.T, radix_sin.T], 0)
    block_cos, block_sin = unit_wave(jnp.arange(block_size, dtype=jnp.int32)[:, None], jnp.arange(block_size, dtype=jnp.int32)[None, :], block_size)
    block_cos = block_cos.astype(jnp.bfloat16)
    block_sin = block_sin.astype(jnp.bfloat16)
    block_fwd = jnp.stack([jnp.stack([block_cos, block_sin], 1), jnp.stack([-block_sin, block_cos], 1)], 0)
    block_inv = jnp.stack([jnp.stack([block_cos, -block_sin], 1), jnp.stack([block_sin, block_cos], 1)], 0)
    return (radix_fwd, radix_inv, block_fwd, block_inv)

def product(left_side, right_side, conjugate):
    left_re = left_side[..., 0, :, :, :]
    left_im = left_side[..., 1, :, :, :]
    if conjugate:
        left_im = -left_im
    right_re = right_side[..., 0, :, :, :]
    right_im = right_side[..., 1, :, :, :]
    joined = jnp.stack([left_re * right_re - left_im * right_im, left_re * right_im + left_im * right_re], -4)
    return joined.astype(jnp.bfloat16)

def forward(signal_in, tables, twiddle):
    radix_fwd = tables[0].astype(jnp.float32)
    block_fwd = tables[2].astype(jnp.float32)
    row_count = tables[0].shape[1]
    grid_in = signal_in.reshape(row_count, BLOCK, -1).astype(jnp.float32)
    first_section = jnp.einsum('odk,djc->okjc', radix_fwd, grid_in, precision=lax.Precision.HIGHEST)
    turned_re = first_section[0] * twiddle[0] - first_section[1] * twiddle[1]
    turned_im = first_section[0] * twiddle[1] + first_section[1] * twiddle[0]
    turned = jnp.stack([turned_re, turned_im], 0).astype(jnp.bfloat16)
    return jnp.einsum('rjoq,rkjc->okqc', block_fwd, turned.astype(jnp.float32), precision=lax.Precision.HIGHEST)

def inverse(spectrum_in, tables, twiddle):
    radix_inv = tables[1].astype(jnp.float32)
    block_inv = tables[3].astype(jnp.float32)
    back_section = jnp.einsum('rqoj,rkqc->okjc', block_inv, spectrum_in.astype(jnp.float32), precision=lax.Precision.HIGHEST)
    unturned_re = back_section[0] * twiddle[0] + back_section[1] * twiddle[1]
    unturned_im = back_section[1] * twiddle[0] - back_section[0] * twiddle[1]
    unturned = jnp.stack([unturned_re, unturned_im], 0).astype(jnp.bfloat16)
    grid_out = jnp.einsum('rkd,rkjc->djc', radix_inv, unturned.astype(jnp.float32), precision=lax.Precision.HIGHEST) * (1.0 / POINTS)
    return grid_out.reshape(LENGTH, -1).astype(jnp.bfloat16)

def reference(value_in, key_in, query_in, filter_taps, out_weight, cotangent):
    row_count = LENGTH // BLOCK
    tables = spectral_tables(row_count, BLOCK)
    wave_cos, wave_sin = unit_wave(jnp.arange(RADIX, dtype=jnp.int32)[:, None], jnp.arange(BLOCK, dtype=jnp.int32)[None, :], POINTS)
    twiddle = (wave_cos[:, :, None], wave_sin[:, :, None])
    gated = (key_in.astype(jnp.float32) * value_in.astype(jnp.float32)).astype(jnp.bfloat16)
    d_gate = cotangent.astype(jnp.float32)
    d_conv = (d_gate * query_in.astype(jnp.float32)).astype(jnp.bfloat16)
    group_size = math.gcd(CH, 128)
    group_count = CH // group_size

    def split_channels(values_in):
        shaped = values_in.reshape(values_in.shape[:-1] + (group_count, group_size))
        return jnp.moveaxis(shaped, -2, 0)

    def join_channels(values_in):
        moved = jnp.moveaxis(values_in, 0, -2)
        return moved.reshape(moved.shape[:-2] + (CH,))

    def transform_one(signal_in):
        return forward(signal_in, tables, twiddle)

    def invert_one(spectrum_in):
        return inverse(spectrum_in, tables, twiddle)

    def per_group(inputs):
        gated_part, dconv_part, taps_part = inputs
        spec_gated = jax.vmap(transform_one)(gated_part)
        spec_taps = transform_one(taps_part)[None]
        spec_dconv = jax.vmap(transform_one)(dconv_part)
        conv = jax.vmap(invert_one)(product(spec_gated, spec_taps, False))
        grad_gated = jax.vmap(invert_one)(product(spec_taps, spec_dconv, True))
        filter_terms = jax.vmap(invert_one)(product(spec_gated, spec_dconv, True))
        return (conv, grad_gated, lax.optimization_barrier(jnp.sum(filter_terms.astype(jnp.float32), 0)))
    conv_parts, grad_parts, filter_parts = lax.map(per_group, (split_channels(gated), split_channels(d_conv), split_channels(filter_taps)))
    conv = join_channels(conv_parts)
    grad_gated = join_channels(grad_parts)
    filter_sum = join_channels(filter_parts)
    loss_scale = 1.0 / math.sqrt(SEQ * LENGTH)
    gate_out = (query_in.astype(jnp.float32) * conv.astype(jnp.float32)).astype(jnp.bfloat16)
    mixed_out = jnp.dot(gate_out.reshape(-1, CH), out_weight, preferred_element_type=jnp.float32).astype(jnp.bfloat16).reshape(SEQ, LENGTH, CH)
    grad_query = (d_gate * conv.astype(jnp.float32)).astype(jnp.bfloat16)
    grad_value = (grad_gated.astype(jnp.float32) * key_in.astype(jnp.float32)).astype(jnp.bfloat16)
    grad_key = (grad_gated.astype(jnp.float32) * value_in.astype(jnp.float32)).astype(jnp.bfloat16)
    grad_filter = filter_sum * loss_scale
    return (mixed_out, grad_value, grad_key, grad_query, grad_filter)
```

```python
import functools
import math

import jax
import jax.numpy as jnp
import numpy as np
from jax import lax
from jax.experimental import pallas as pl
from jax.experimental.pallas import tpu as pltpu
from jax.sharding import PartitionSpec as P

LANES = 128
F32 = jnp.float32
BF16 = jnp.bfloat16


def right_angle_tables(source_count, length):
    radix = length // LANES
    quarters = radix // source_count
    row = np.arange(radix)
    slow = (row % source_count) * quarters + row // source_count
    freq = np.arange(radix) + 0.25
    slow_angle = -2.0 * np.pi * freq[:, None] * slow[None, :] / radix
    slow_fwd = np.concatenate([np.cos(slow_angle), np.sin(slow_angle)], 0)
    slow_inv = slow_fwd.T
    fast = np.arange(LANES)
    turn_angle = -2.0 * np.pi * freq[:, None] * fast[None, :] / length
    turn_cos, turn_sin = np.cos(turn_angle), np.sin(turn_angle)
    fast_angle = -2.0 * np.pi * ((fast[:, None] * fast[None, :]) % LANES) / LANES
    fast_cos, fast_sin = np.cos(fast_angle), np.sin(fast_angle)
    fast_fwd = np.block([[fast_cos, fast_sin], [-fast_sin, fast_cos]])
    fast_inv = np.block([[fast_cos, -fast_sin], [fast_sin, fast_cos]])
    turn = np.stack([turn_cos, turn_sin, turn_cos / length, turn_sin / length])
    return (
        jnp.asarray(slow_fwd, BF16),
        jnp.asarray(fast_fwd, BF16),
        jnp.asarray(fast_inv, BF16),
        jnp.asarray(slow_inv, BF16),
        jnp.asarray(turn, F32),
    )


def dot(left, right):
    return jnp.dot(left, right, preferred_element_type=F32)


def flip(square):
    extent = square.shape[1]
    rows = lax.broadcasted_iota(jnp.int32, (extent, extent), 0)
    cols = lax.broadcasted_iota(jnp.int32, (extent, extent), 1)
    unit = jnp.where(rows == cols, 1.0, 0.0).astype(BF16)
    turned = lax.dot_general(unit, square, (((1,), (1,)), ((), ())), preferred_element_type=F32)
    return turned.astype(BF16)


def times(left, right):
    return (left.astype(F32) * right.astype(F32)).astype(BF16)


def gate_kernel(value_ref, key_ref, query_ref, cot_ref, taps_ref, out_ref):
    group = out_ref.shape[1] // 3
    signals = (
        times(key_ref[...], value_ref[...]),
        taps_ref[...],
        times(cot_ref[...], query_ref[...]),
    )
    for slot, signal in enumerate(signals):
        turned = flip(signal)
        out_ref[:, slot * group : (slot + 1) * group, :] = turned.reshape(
            out_ref.shape[0], group, turned.shape[1]
        )


def spread(in_ref, first_row, wide_ref, group):
    for source in range(in_ref.shape[0]):
        rows = in_ref[source, first_row : first_row + group, :].astype(F32)
        for quarter in range(wide_ref.shape[0]):
            wide_ref[quarter, source * group : (source + 1) * group, :] = rows[
                :, quarter * LANES : (quarter + 1) * LANES
            ]


def forward_pair(wide_ref, chan, group, tables):
    slow_fwd, fast_fwd, _, _, turn = tables
    quarters, rows, _ = wide_ref.shape
    columns = [
        jnp.concatenate(
            [wide_ref[q, pl.ds(one, rows // group, stride=group), :] for q in range(quarters)], 0
        )
        for one in (chan, chan + 1)
    ]
    first = dot(slow_fwd[...], jnp.concatenate(columns, 1).astype(BF16))
    radix = first.shape[0] // 2
    turn_cos, turn_sin = turn[0], turn[1]
    sides = []
    for side in range(2):
        lanes = slice(side * LANES, (side + 1) * LANES)
        part_re, part_im = first[:radix, lanes], first[radix:, lanes]
        sides.append(
            jnp.concatenate(
                [
                    (part_re * turn_cos - part_im * turn_sin).astype(BF16),
                    (part_re * turn_sin + part_im * turn_cos).astype(BF16),
                ],
                1,
            )
        )
    return dot(jnp.concatenate(sides, 0), fast_fwd[...])


def product(left, right, conjugate):
    left_re, left_im = left[:, :LANES], left[:, LANES:]
    right_re, right_im = right[:, :LANES], right[:, LANES:]
    if conjugate:
        both_re = left_re * right_re + left_im * right_im
        both_im = left_re * right_im - left_im * right_re
    else:
        both_re = left_re * right_re - left_im * right_im
        both_im = left_re * right_im + left_im * right_re
    return jnp.concatenate([both_re, both_im], 1).astype(BF16)


def inverse_pair(spectrum, chan, wide_ref, group, tables):
    _, _, fast_inv, slow_inv, turn = tables
    back = dot(spectrum, fast_inv[...])
    radix = back.shape[0] // 2
    turn_cos, turn_sin = turn[2], turn[3]
    parts_re, parts_im = [], []
    for side in range(2):
        rows = slice(side * radix, (side + 1) * radix)
        back_re, back_im = back[rows, :LANES], back[rows, LANES:]
        parts_re.append((back_re * turn_cos + back_im * turn_sin).astype(BF16))
        parts_im.append((back_im * turn_cos - back_re * turn_sin).astype(BF16))
    unturned = jnp.concatenate(
        [jnp.concatenate(parts_re, 1), jnp.concatenate(parts_im, 1)], 0
    )
    signal = dot(slow_inv[...], unturned)
    quarters, rows, _ = wide_ref.shape
    sources = rows // group
    for side in range(2):
        one = signal[:, side * LANES : (side + 1) * LANES]
        for q in range(quarters):
            wide_ref[q, pl.ds(chan + side, sources, stride=group), :] = one[
                q * sources : (q + 1) * sources
            ]


def collect(wide_ref, out_ref, first_row, group):
    for source in range(out_ref.shape[0]):
        out_ref[source, first_row : first_row + group, :] = jnp.concatenate(
            [
                wide_ref[quarter, source * group : (source + 1) * group, :]
                for quarter in range(wide_ref.shape[0])
            ],
            1,
        ).astype(BF16)


def conv_kernel(in_ref, *refs):
    tables = refs[:5]
    conv_ref, gated_ref, taps_ref, wide_gated, wide_taps, wide_out = refs[5:]
    group = conv_ref.shape[1]
    spread(in_ref, 0, wide_gated, group)
    spread(in_ref, group, wide_taps, group)
    for pair in range(group // 2):
        spec_gated = forward_pair(wide_gated, 2 * pair, group, tables)
        spec_taps = forward_pair(wide_taps, 2 * pair, group, tables)
        gated_ref[pair] = spec_gated
        taps_ref[pair] = spec_taps
        inverse_pair(product(spec_gated, spec_taps, False), 2 * pair, wide_out, group, tables)
    collect(wide_out, conv_ref, 0, group)


def grad_kernel(in_ref, gated_ref, taps_ref, *refs):
    tables = refs[:5]
    terms_ref, grad_ref, wide_dconv, wide_terms, wide_grad = refs[5:]
    group = grad_ref.shape[1]
    spread(in_ref, 2 * group, wide_dconv, group)
    for pair in range(group // 2):
        spec_dconv = forward_pair(wide_dconv, 2 * pair, group, tables)
        inverse_pair(
            product(gated_ref[pair], spec_dconv, True), 2 * pair, wide_terms, group, tables
        )
        inverse_pair(product(taps_ref[pair], spec_dconv, True), 2 * pair, wide_grad, group, tables)
    collect(wide_terms, terms_ref, 0, group)
    collect(wide_grad, grad_ref, 0, group)


def project_kernel(
    tensor_ref, conv_ref, query_ref, cot_ref, weight_ref, grad_ref, part_ref, gate_ref
):
    @pl.when(pl.program_id(0) == 0)
    def _():
        conv = flip(conv_ref[...].reshape(-1, conv_ref.shape[-1]))
        grad_ref[...] = times(cot_ref[...], conv)
        gate_ref[...] = times(query_ref[...], conv)

    part_ref[...] = dot(gate_ref[...], weight_ref[...]).astype(BF16)


def finish_kernel(scale, in_ref, key_ref, value_ref, value_grad_ref, key_grad_ref, taps_grad_ref):
    group = in_ref.shape[1] // 2
    grad = flip(in_ref[:, :group, :].reshape(-1, in_ref.shape[-1]))
    value_grad_ref[...] = times(grad, key_ref[...])
    key_grad_ref[...] = times(grad, value_ref[...])
    terms = flip(in_ref[:, group:, :].reshape(-1, in_ref.shape[-1]))
    taps_grad_ref[...] = terms.astype(F32) * scale


VMEM = pl.BlockSpec(memory_space=pltpu.VMEM)


def params():
    return pltpu.CompilerParams(vmem_limit_bytes=48 * 1024 * 1024)


def cost(flops, moved):
    return pl.CostEstimate(flops=flops, bytes_accessed=moved, transcendentals=0)


def shards(value_in, key_in, query_in, filter_taps, out_weight, cotangent):
    _, block, chans = value_in.shape
    sources = lax.axis_size("context")
    tensors = lax.axis_size("tensor")
    length = sources * block
    group = chans // sources
    radix = length // LANES
    value_in, key_in, query_in, cotangent = (
        one.reshape(block, chans) for one in (value_in, key_in, query_in, cotangent)
    )
    tables = right_angle_tables(sources, length)

    steps = chans // LANES
    slab = pl.BlockSpec((block, LANES), lambda step: (0, step))
    sent = pl.pallas_call(
        gate_kernel,
        grid=(steps,),
        in_specs=[slab] * 5,
        out_specs=pl.BlockSpec((sources // steps, 3 * group, block), lambda step: (step, 0, 0)),
        out_shape=jax.ShapeDtypeStruct((sources, 3 * group, block), BF16),
        compiler_params=params(),
        cost_estimate=cost(6 * block * chans * LANES, 8 * 2 * block * chans),
        name="gate_and_turn",
    )(value_in, key_in, query_in, cotangent, filter_taps)
    received = lax.all_to_all(sent, "context", 0, 0, tiled=True)

    piece = jax.ShapeDtypeStruct((sources, group, block), BF16)
    spectrum = jax.ShapeDtypeStruct((group // 2, 2 * radix, 2 * LANES), F32)
    wide = pltpu.VMEM((block // LANES, sources * group, LANES), F32)
    work = 6 * group * radix * LANES * 4 * LANES
    conv, spec_gated, spec_taps = pl.pallas_call(
        conv_kernel,
        in_specs=[VMEM] * 6,
        out_specs=[VMEM] * 3,
        out_shape=[piece, spectrum, spectrum],
        scratch_shapes=[wide] * 3,
        compiler_params=params(),
        cost_estimate=cost(work, 8 * 2**20),
        name="convolve",
    )(received, *tables)
    conv_back = lax.all_to_all(conv, "context", 0, 0, tiled=True)
    terms, grad = pl.pallas_call(
        grad_kernel,
        in_specs=[VMEM] * 8,
        out_specs=[VMEM] * 2,
        out_shape=[piece, piece],
        scratch_shapes=[wide] * 3,
        compiler_params=params(),
        cost_estimate=cost(work, 8 * 2**20),
        name="correlate",
    )(received, spec_gated, spec_taps, *tables)
    others = lax.ppermute(terms, "dp", [(0, 1), (1, 0)])

    where = lax.axis_index("tensor").astype(jnp.int32).reshape(1)
    grad_query, parts = pl.pallas_call(
        project_kernel,
        grid_spec=pltpu.PrefetchScalarGridSpec(
            num_scalar_prefetch=1,
            grid=(tensors,),
            in_specs=[
                pl.BlockSpec((sources, group, block), lambda step, at: (0, 0, 0)),
                pl.BlockSpec((block, chans), lambda step, at: (0, 0)),
                pl.BlockSpec((block, chans), lambda step, at: (0, 0)),
                pl.BlockSpec((chans, chans), lambda step, at: (0, (at[0] + step) % tensors)),
            ],
            out_specs=[
                pl.BlockSpec((block, chans), lambda step, at: (0, 0)),
                pl.BlockSpec((None, block, chans), lambda step, at: (step, 0, 0)),
            ],
            scratch_shapes=[pltpu.VMEM((block, chans), BF16)],
        ),
        out_shape=[
            jax.ShapeDtypeStruct((block, chans), BF16),
            jax.ShapeDtypeStruct((tensors, block, chans), BF16),
        ],
        compiler_params=params(),
        cost_estimate=cost(2 * block * chans * chans * tensors, 6 * 2**20),
        name="project",
    )(where, conv_back, query_in, cotangent, out_weight)
    total = parts[0].astype(F32)
    for offset in range(1, tensors):
        total = total + lax.ppermute(
            parts[offset], "tensor", [(one, (one + offset) % tensors) for one in range(tensors)]
        ).astype(F32)
    mixed_out = total.astype(BF16)

    terms_sum = (terms.astype(F32) + others.astype(F32)).astype(BF16)
    grads_back = lax.all_to_all(
        jnp.concatenate([grad, terms_sum], 1), "context", 0, 0, tiled=True
    )
    scale = 1.0 / math.sqrt(lax.axis_size("dp") * length)
    steps = block // LANES
    slab = pl.BlockSpec((LANES, chans), lambda step: (step, 0))
    grad_value, grad_key, grad_filter = pl.pallas_call(
        functools.partial(finish_kernel, scale),
        grid=(steps,),
        in_specs=[
            pl.BlockSpec((sources, 2 * group, LANES), lambda step: (0, 0, step)),
            slab,
            slab,
        ],
        out_specs=[slab] * 3,
        out_shape=[
            jax.ShapeDtypeStruct((block, chans), BF16),
            jax.ShapeDtypeStruct((block, chans), BF16),
            jax.ShapeDtypeStruct((block, chans), F32),
        ],
        compiler_params=params(),
        cost_estimate=cost(4 * block * chans * LANES, 10 * block * chans),
        name="finish",
    )(grads_back, key_in, value_in)
    return (
        mixed_out[None],
        grad_value[None],
        grad_key[None],
        grad_query[None],
        grad_filter,
    )


def solution(mesh):
    whole = P("dp", "context", "tensor")
    return jax.shard_map(
        shards,
        mesh=mesh,
        in_specs=(whole, whole, whole, P("context", "tensor"), P("tensor", None), whole),
        out_specs=(whole, whole, whole, whole, P("context", "tensor")),
        check_vma=False,
    )
```

```python
import functools
import math

import jax
import jax.numpy as jnp
import numpy as np
from jax import lax
from jax.experimental import pallas as pl
from jax.experimental.pallas import tpu as pltpu
from jax.sharding import PartitionSpec as P

LANES = 128
F32 = jnp.float32
BF16 = jnp.bfloat16
SMALL = 16
MIDDLE = 36
ADD = 60
PROJECT = 60


def right_angle_tables(source_count, length):
    radix = length // LANES
    quarters = radix // source_count
    row = np.arange(radix)
    slow = (row % source_count) * quarters + row // source_count
    freq = np.arange(radix) + 0.25
    slow_angle = -2.0 * np.pi * freq[:, None] * slow[None, :] / radix
    slow_fwd = np.concatenate([np.cos(slow_angle), np.sin(slow_angle)], 0)
    slow_inv = slow_fwd.T
    fast = np.arange(LANES)
    turn_angle = -2.0 * np.pi * freq[:, None] * fast[None, :] / length
    turn_cos, turn_sin = np.cos(turn_angle), np.sin(turn_angle)
    fast_angle = -2.0 * np.pi * ((fast[:, None] * fast[None, :]) % LANES) / LANES
    fast_cos, fast_sin = np.cos(fast_angle), np.sin(fast_angle)
    fast_fwd = np.block([[fast_cos, fast_sin], [-fast_sin, fast_cos]])
    fast_inv = np.block([[fast_cos, -fast_sin], [fast_sin, fast_cos]])
    turn = np.stack([turn_cos, turn_sin, turn_cos / length, turn_sin / length])
    slow_fwd = np.concatenate([slow_fwd, np.zeros_like(slow_fwd)], 1)
    factors = np.concatenate([slow_fwd, fast_fwd, fast_inv, slow_inv], 0)
    return (jnp.asarray(factors, BF16), jnp.asarray(turn, F32))


def factors_of(factors_ref):
    size = 2 * LANES
    return (
        factors_ref.at[:size, :LANES],
        factors_ref.at[size : 2 * size, :],
        factors_ref.at[2 * size : 3 * size, :],
        factors_ref.at[3 * size :, :],
    )


def dot(left, right):
    return jnp.dot(left, right, preferred_element_type=F32)


def flip(square):
    extent = square.shape[1]
    rows = lax.broadcasted_iota(jnp.int32, (extent, extent), 0)
    cols = lax.broadcasted_iota(jnp.int32, (extent, extent), 1)
    unit = jnp.where(rows == cols, 1.0, 0.0).astype(BF16)
    turned = lax.dot_general(unit, square, (((1,), (1,)), ((), ())), preferred_element_type=F32)
    return turned.astype(BF16)


def times(left, right):
    return (left.astype(F32) * right.astype(F32)).astype(BF16)


def gate_kernel(*refs):
    in_refs, (out_ref, held, arrival) = refs[:5], refs[5:]
    _, chunks, _, width = held.shape

    def copy(one, chunk):
        return pltpu.make_async_copy(
            in_refs[one].at[:, pl.ds(chunk * width, width)],
            held.at[one, chunk],
            arrival.at[one, chunk],
        )

    for chunk in range(chunks):
        for one in range(5):
            copy(one, chunk).start()
    group = out_ref.shape[1] // 3
    share = out_ref.shape[0] // chunks
    for chunk in range(chunks):
        for one in range(5):
            copy(one, chunk).wait()
        value, key, query, cotangent, taps = (held[one, chunk] for one in range(5))
        for slot, signal in enumerate((times(key, value), taps, times(cotangent, query))):
            turned = flip(signal)
            out_ref[
                chunk * share : (chunk + 1) * share, slot * group : (slot + 1) * group, :
            ] = turned.reshape(share, group, turned.shape[1])


def spread(in_ref, first_row, wide_ref, group):
    for source in range(in_ref.shape[0]):
        rows = in_ref[source, first_row : first_row + group, :].astype(F32)
        for quarter in range(wide_ref.shape[0]):
            wide_ref[quarter, source * group : (source + 1) * group, :] = rows[
                :, quarter * LANES : (quarter + 1) * LANES
            ]


def turn_forward(wide_ref, turned_ref, group, slow_fwd, turn):
    quarters, rows, _ = wide_ref.shape
    turn_cos, turn_sin = turn[0], turn[1]
    for chan in range(0, group, 2):
        columns = [
            jnp.concatenate(
                [wide_ref[q, pl.ds(one, rows // group, stride=group), :] for q in range(quarters)],
                0,
            )
            for one in (chan, chan + 1)
        ]
        first = dot(slow_fwd[...], jnp.concatenate(columns, 1).astype(BF16))
        radix = first.shape[0] // 2
        for side in range(2):
            lanes = slice(side * LANES, (side + 1) * LANES)
            part_re, part_im = first[:radix, lanes], first[radix:, lanes]
            out_rows = slice((chan + side) * radix, (chan + side + 1) * radix)
            turned_ref[out_rows, :LANES] = (part_re * turn_cos - part_im * turn_sin).astype(BF16)
            turned_ref[out_rows, LANES:] = (part_re * turn_sin + part_im * turn_cos).astype(BF16)


def product(left, right, conjugate):
    left_re, left_im = left[:, :LANES], left[:, LANES:]
    right_re, right_im = right[:, :LANES], right[:, LANES:]
    if conjugate:
        both_re = left_re * right_re + left_im * right_im
        both_im = left_re * right_im - left_im * right_re
    else:
        both_re = left_re * right_re - left_im * right_im
        both_im = left_re * right_im + left_im * right_re
    return jnp.concatenate([both_re, both_im], 1).astype(BF16)


def invert(spectrum_ref, back_ref, wide_ref, group, fast_inv, slow_inv, turn):
    back_ref[...] = dot(spectrum_ref[...], fast_inv[...])
    quarters, rows, _ = wide_ref.shape
    sources = rows // group
    radix = back_ref.shape[0] // group
    turn_cos, turn_sin = turn[2], turn[3]
    for chan in range(0, group, 2):
        parts_re, parts_im = [], []
        for one in (chan, chan + 1):
            in_rows = slice(one * radix, (one + 1) * radix)
            back_re, back_im = back_ref[in_rows, :LANES], back_ref[in_rows, LANES:]
            parts_re.append((back_re * turn_cos + back_im * turn_sin).astype(BF16))
            parts_im.append((back_im * turn_cos - back_re * turn_sin).astype(BF16))
        unturned = jnp.concatenate(
            [jnp.concatenate(parts_re, 1), jnp.concatenate(parts_im, 1)], 0
        )
        signal = dot(slow_inv[...], unturned)
        for side in range(2):
            one = signal[:, side * LANES : (side + 1) * LANES]
            for q in range(quarters):
                wide_ref[q, pl.ds(chan + side, sources, stride=group), :] = one[
                    q * sources : (q + 1) * sources
                ]


def collect(wide_ref, out_ref, group):
    for source in range(out_ref.shape[0]):
        out_ref[source, :group, :] = jnp.concatenate(
            [
                wide_ref[quarter, source * group : (source + 1) * group, :]
                for quarter in range(wide_ref.shape[0])
            ],
            1,
        ).astype(BF16)


def transform_kernel(in_ref, factors_ref, turn, *refs):
    slow_fwd, fast_fwd, fast_inv, slow_inv = factors_of(factors_ref)
    out_refs, (wide, turned, spectra, mixed, back) = refs[:3], refs[3:]
    group = out_refs[0].shape[1]
    for slot in range(3):
        spread(in_ref, slot * group, wide.at[slot], group)
        turn_forward(wide.at[slot], turned.at[slot], group, slow_fwd, turn)
        spectra[slot] = dot(turned[slot], fast_fwd[...])
    rows = spectra.shape[1] // group
    for chan in range(group):
        part = slice(chan * rows, (chan + 1) * rows)
        gated, taps, dconv = (spectra[slot, part, :] for slot in range(3))
        mixed[0, part, :] = product(gated, taps, False)
        mixed[1, part, :] = product(gated, dconv, True)
        mixed[2, part, :] = product(taps, dconv, True)
    for slot, out_ref in enumerate(out_refs):
        invert(mixed.at[slot], back.at[slot], wide.at[slot], group, fast_inv, slow_inv, turn)
        collect(wide.at[slot], out_ref, group)


def add_kernel(*refs):
    total = refs[0][...].astype(F32)
    for one in refs[1:-1]:
        total = total + one[...].astype(F32)
    refs[-1][...] = total.astype(BF16)


def join_kernel(upper_ref, lower_ref, out_ref):
    group = upper_ref.shape[1]
    out_ref[:, :group, :] = upper_ref[...]
    out_ref[:, group:, :] = lower_ref[...]


def project_kernel(order_ref, conv_ref, query_ref, cot_ref, weight_ref, *out_refs):
    chans = query_ref.shape[1]
    gates = []
    for step in range(query_ref.shape[0] // LANES):
        rows = slice(step * LANES, (step + 1) * LANES)
        conv = flip(conv_ref[:, :, rows].reshape(-1, LANES))
        out_refs[4][rows, :] = times(cot_ref[rows, :], conv)
        gates.append(times(query_ref[rows, :], conv))
    for slot in range(4):
        columns = pl.ds(pl.multiple_of(order_ref[slot] * chans, chans), chans)
        for step, gate_out in enumerate(gates):
            rows = slice(step * LANES, (step + 1) * LANES)
            out_refs[slot][rows, :] = dot(gate_out, weight_ref[:, columns]).astype(BF16)


def finish_kernel(scale, in_ref, key_ref, value_ref, value_grad_ref, key_grad_ref, taps_grad_ref):
    group = in_ref.shape[1] // 2
    grad = flip(in_ref[:, :group, :].reshape(-1, in_ref.shape[-1]))
    value_grad_ref[...] = times(grad, key_ref[...])
    key_grad_ref[...] = times(grad, value_ref[...])
    terms = flip(in_ref[:, group:, :].reshape(-1, in_ref.shape[-1]))
    taps_grad_ref[...] = terms.astype(F32) * scale


VMEM = pl.BlockSpec(memory_space=pltpu.VMEM)
HBM = pl.BlockSpec(memory_space=pltpu.HBM)


def params(mebibytes=60):
    return pltpu.CompilerParams(vmem_limit_bytes=mebibytes * 1024 * 1024)


def cost(flops, moved):
    return pl.CostEstimate(flops=flops, bytes_accessed=moved, transcendentals=0)


def add_arrays(arrays, flops, name):
    return pl.pallas_call(
        add_kernel,
        in_specs=[VMEM] * len(arrays),
        out_specs=VMEM,
        out_shape=jax.ShapeDtypeStruct(arrays[0].shape, BF16),
        compiler_params=params(SMALL),
        cost_estimate=cost(flops, 2 * arrays[0].size * (len(arrays) + 1)),
        name=name,
    )(*arrays)


def shards(value_in, key_in, query_in, filter_taps, out_weight, cotangent):
    _, block, chans = value_in.shape
    sources = lax.axis_size("context")
    tensors = lax.axis_size("tensor")
    length = sources * block
    group = chans // sources
    radix = length // LANES
    value_in, key_in, query_in, cotangent = (
        one.reshape(block, chans) for one in (value_in, key_in, query_in, cotangent)
    )
    tables = right_angle_tables(sources, length)

    steps = chans // LANES
    sent = pl.pallas_call(
        gate_kernel,
        in_specs=[HBM] * 5,
        out_specs=VMEM,
        out_shape=jax.ShapeDtypeStruct((sources, 3 * group, block), BF16),
        scratch_shapes=[
            pltpu.VMEM((5, steps, block, LANES), BF16),
            pltpu.SemaphoreType.DMA((5, steps)),
        ],
        compiler_params=params(),
        cost_estimate=cost(6 * block * chans * LANES, 8 * 2 * block * chans),
        name="gate_and_turn",
    )(value_in, key_in, query_in, cotangent, filter_taps)
    received = lax.all_to_all(sent, "context", 0, 0, tiled=True)

    piece = jax.ShapeDtypeStruct((sources, group, block), BF16)
    rows = group * radix
    spectrum = (rows, 2 * LANES)
    wide = (block // LANES, sources * group, LANES)
    work = 6 * group * radix * LANES * 4 * LANES
    conv, terms, grad = pl.pallas_call(
        transform_kernel,
        in_specs=[VMEM] * 3,
        out_specs=[VMEM] * 3,
        out_shape=[piece] * 3,
        scratch_shapes=[
            pltpu.VMEM((3,) + wide, F32),
            pltpu.VMEM((3,) + spectrum, BF16),
            pltpu.VMEM((3,) + spectrum, F32),
            pltpu.VMEM((3,) + spectrum, BF16),
            pltpu.VMEM((3,) + spectrum, F32),
        ],
        compiler_params=params(MIDDLE),
        cost_estimate=cost(work, 8 * 2**20),
        name="transform",
    )(received, *tables)
    conv_back = lax.all_to_all(conv, "context", 0, 0, tiled=True)
    others = lax.ppermute(terms, "dp", [(0, 1), (1, 0)])

    at = lax.axis_index("tensor").astype(jnp.int32)
    last = tensors - 1
    mirrored = at > last - at

    def toward(chunk):
        return jnp.where(mirrored, last - chunk, chunk)

    outer = (at == 0) | (at == last)
    order = jnp.stack(
        [
            toward(3),
            jnp.where(outer, toward(1), toward(2)),
            jnp.where(outer, toward(2), toward(0)),
            at,
        ]
    )
    steps = block // LANES
    square = jax.ShapeDtypeStruct((block, chans), BF16)
    slab = pl.BlockSpec((LANES, chans), lambda step: (step, 0))
    far, near, other, own, grad_query = pl.pallas_call(
        project_kernel,
        in_specs=[pl.BlockSpec(memory_space=pltpu.SMEM)] + [VMEM] * 4,
        out_specs=[VMEM] * 5,
        out_shape=[square] * 5,
        compiler_params=params(SMALL),
        cost_estimate=cost(2 * block * chans * chans * tensors, 6 * 2**20),
        name="project",
    )(order, conv_back, query_in, cotangent, out_weight)
    relayed = lax.ppermute(far, "tensor", [(0, 1), (3, 2)])
    across = lax.ppermute(near, "tensor", [(1, 2), (2, 1)])
    beside = lax.ppermute(other, "tensor", [(0, 2), (3, 1), (1, 0), (2, 3)])
    inward = lax.ppermute(near, "tensor", [(0, 1), (3, 2)])
    terms_sum = add_arrays((terms, others), 2 * 10**9, "sum_terms")
    terms_sum, relayed = lax.optimization_barrier((terms_sum, relayed))
    both = add_arrays((far, relayed), 10**11, "relay")
    terms_sum, both = lax.optimization_barrier((terms_sum, both))
    outward = lax.ppermute(both, "tensor", [(1, 3), (2, 0)])
    joined = pl.pallas_call(
        join_kernel,
        in_specs=[VMEM] * 2,
        out_specs=VMEM,
        out_shape=jax.ShapeDtypeStruct((sources, 2 * group, block), BF16),
        compiler_params=params(SMALL),
        cost_estimate=cost(10**11, 4 * 2 * block * chans),
        name="join",
    )(grad, terms_sum)
    mixed_out = add_arrays(
        (own, across, beside, inward, outward), 10**11, "add_parts"
    )
    grads_back = lax.all_to_all(joined, "context", 0, 0, tiled=True)
    scale = 1.0 / math.sqrt(lax.axis_size("dp") * length)
    grad_value, grad_key, grad_filter = pl.pallas_call(
        functools.partial(finish_kernel, scale),
        grid=(steps,),
        in_specs=[
            pl.BlockSpec((sources, 2 * group, LANES), lambda step: (0, 0, step)),
            slab,
            slab,
        ],
        out_specs=[slab] * 3,
        out_shape=[
            jax.ShapeDtypeStruct((block, chans), BF16),
            jax.ShapeDtypeStruct((block, chans), BF16),
            jax.ShapeDtypeStruct((block, chans), F32),
        ],
        compiler_params=params(SMALL),
        cost_estimate=cost(4 * block * chans * LANES, 10 * block * chans),
        name="finish",
    )(grads_back, key_in, value_in)
    return (
        mixed_out[None],
        grad_value[None],
        grad_key[None],
        grad_query[None],
        grad_filter,
    )


def solution(mesh):
    whole = P("dp", "context", "tensor")
    return jax.shard_map(
        shards,
        mesh=mesh,
        in_specs=(whole, whole, whole, P("context", "tensor"), P("tensor", None), whole),
        out_specs=(whole, whole, whole, whole, P("context", "tensor")),
        check_vma=False,
    )
```

```python
import functools
import math

import jax
import jax.numpy as jnp
import numpy as np
from jax import lax
from jax.experimental import pallas as pl
from jax.experimental.pallas import tpu as pltpu
from jax.sharding import PartitionSpec as P

LANES = 128
F32 = jnp.float32
BF16 = jnp.bfloat16
SMALL = 16
MIDDLE = 36
ADD = 60
PROJECT = 60


def right_angle_tables(source_count, length):
    radix = length // LANES
    quarters = radix // source_count
    row = np.arange(radix)
    slow = (row % source_count) * quarters + row // source_count
    freq = np.arange(radix) + 0.25
    slow_angle = -2.0 * np.pi * freq[:, None] * slow[None, :] / radix
    slow_fwd = np.concatenate([np.cos(slow_angle), np.sin(slow_angle)], 0)
    slow_inv = slow_fwd.T
    fast = np.arange(LANES)
    turn_angle = -2.0 * np.pi * freq[:, None] * fast[None, :] / length
    turn_cos, turn_sin = np.cos(turn_angle), np.sin(turn_angle)
    fast_angle = -2.0 * np.pi * ((fast[:, None] * fast[None, :]) % LANES) / LANES
    fast_cos, fast_sin = np.cos(fast_angle), np.sin(fast_angle)
    fast_fwd = np.block([[fast_cos, fast_sin], [-fast_sin, fast_cos]])
    fast_inv = np.block([[fast_cos, -fast_sin], [fast_sin, fast_cos]])
    turn = np.stack([turn_cos, turn_sin, turn_cos / length, turn_sin / length])
    slow_fwd = np.concatenate([slow_fwd, np.zeros_like(slow_fwd)], 1)
    factors = np.concatenate([slow_fwd, fast_fwd, fast_inv, slow_inv], 0)
    return (jnp.asarray(factors, BF16), jnp.asarray(turn, F32))


def factors_of(factors_ref):
    size = 2 * LANES
    return (
        factors_ref.at[:size, :LANES],
        factors_ref.at[size : 2 * size, :],
        factors_ref.at[2 * size : 3 * size, :],
        factors_ref.at[3 * size :, :],
    )


def dot(left, right):
    return jnp.dot(left, right, preferred_element_type=F32)


def flip(square):
    extent = square.shape[1]
    rows = lax.broadcasted_iota(jnp.int32, (extent, extent), 0)
    cols = lax.broadcasted_iota(jnp.int32, (extent, extent), 1)
    unit = jnp.where(rows == cols, 1.0, 0.0).astype(BF16)
    turned = lax.dot_general(unit, square, (((1,), (1,)), ((), ())), preferred_element_type=F32)
    return turned.astype(BF16)


def times(left, right):
    return (left.astype(F32) * right.astype(F32)).astype(BF16)


def gate_kernel(*refs):
    in_refs, (out_ref, held, arrival) = refs[:5], refs[5:]
    _, chunks, _, width = held.shape

    def copy(one, chunk):
        return pltpu.make_async_copy(
            in_refs[one].at[:, pl.ds(chunk * width, width)],
            held.at[one, chunk],
            arrival.at[one, chunk],
        )

    for chunk in range(chunks):
        for one in range(5):
            copy(one, chunk).start()
    group = out_ref.shape[1] // 3
    share = out_ref.shape[0] // chunks
    for chunk in range(chunks):
        for one in range(5):
            copy(one, chunk).wait()
        value, key, query, cotangent, taps = (held[one, chunk] for one in range(5))
        for slot, signal in enumerate((times(key, value), taps, times(cotangent, query))):
            turned = flip(signal)
            out_ref[
                chunk * share : (chunk + 1) * share, slot * group : (slot + 1) * group, :
            ] = turned.reshape(share, group, turned.shape[1])


def spread(in_ref, first_row, wide_ref, group):
    for source in range(in_ref.shape[0]):
        rows = in_ref[source, first_row : first_row + group, :].astype(F32)
        for quarter in range(wide_ref.shape[0]):
            wide_ref[quarter, source * group : (source + 1) * group, :] = rows[
                :, quarter * LANES : (quarter + 1) * LANES
            ]


def turn_forward(wide_ref, turned_ref, group, slow_fwd, turn):
    quarters, rows, _ = wide_ref.shape
    turn_cos, turn_sin = turn[0], turn[1]
    for chan in range(0, group, 2):
        columns = [
            jnp.concatenate(
                [wide_ref[q, pl.ds(one, rows // group, stride=group), :] for q in range(quarters)],
                0,
            )
            for one in (chan, chan + 1)
        ]
        first = dot(slow_fwd[...], jnp.concatenate(columns, 1).astype(BF16))
        radix = first.shape[0] // 2
        for side in range(2):
            lanes = slice(side * LANES, (side + 1) * LANES)
            part_re, part_im = first[:radix, lanes], first[radix:, lanes]
            out_rows = slice((chan + side) * radix, (chan + side + 1) * radix)
            turned_ref[out_rows, :LANES] = (part_re * turn_cos - part_im * turn_sin).astype(BF16)
            turned_ref[out_rows, LANES:] = (part_re * turn_sin + part_im * turn_cos).astype(BF16)


def product(left, right, conjugate):
    left_re, left_im = left[:, :LANES], left[:, LANES:]
    right_re, right_im = right[:, :LANES], right[:, LANES:]
    if conjugate:
        both_re = left_re * right_re + left_im * right_im
        both_im = left_re * right_im - left_im * right_re
    else:
        both_re = left_re * right_re - left_im * right_im
        both_im = left_re * right_im + left_im * right_re
    return jnp.concatenate([both_re, both_im], 1).astype(BF16)


def invert(spectrum_ref, back_ref, wide_ref, group, fast_inv, slow_inv, turn):
    back_ref[...] = dot(spectrum_ref[...], fast_inv[...])
    quarters, rows, _ = wide_ref.shape
    sources = rows // group
    radix = back_ref.shape[0] // group
    turn_cos, turn_sin = turn[2], turn[3]
    for chan in range(0, group, 2):
        parts_re, parts_im = [], []
        for one in (chan, chan + 1):
            in_rows = slice(one * radix, (one + 1) * radix)
            back_re, back_im = back_ref[in_rows, :LANES], back_ref[in_rows, LANES:]
            parts_re.append((back_re * turn_cos + back_im * turn_sin).astype(BF16))
            parts_im.append((back_im * turn_cos - back_re * turn_sin).astype(BF16))
        unturned = jnp.concatenate(
            [jnp.concatenate(parts_re, 1), jnp.concatenate(parts_im, 1)], 0
        )
        signal = dot(slow_inv[...], unturned)
        for side in range(2):
            one = signal[:, side * LANES : (side + 1) * LANES]
            for q in range(quarters):
                wide_ref[q, pl.ds(chan + side, sources, stride=group), :] = one[
                    q * sources : (q + 1) * sources
                ]


def collect(wide_ref, out_ref, group):
    for source in range(out_ref.shape[0]):
        out_ref[source, :group, :] = jnp.concatenate(
            [
                wide_ref[quarter, source * group : (source + 1) * group, :]
                for quarter in range(wide_ref.shape[0])
            ],
            1,
        ).astype(BF16)


def transform_kernel(in_ref, factors_ref, turn, *refs):
    slow_fwd, fast_fwd, fast_inv, slow_inv = factors_of(factors_ref)
    out_refs, (wide, turned, spectra, mixed, back) = refs[:3], refs[3:]
    group = out_refs[0].shape[1]
    for slot in range(3):
        spread(in_ref, slot * group, wide.at[slot], group)
        turn_forward(wide.at[slot], turned.at[slot], group, slow_fwd, turn)
        spectra[slot] = dot(turned[slot], fast_fwd[...])
    rows = spectra.shape[1] // group
    for chan in range(group):
        part = slice(chan * rows, (chan + 1) * rows)
        gated, taps, dconv = (spectra[slot, part, :] for slot in range(3))
        mixed[0, part, :] = product(gated, taps, False)
        mixed[1, part, :] = product(gated, dconv, True)
        mixed[2, part, :] = product(taps, dconv, True)
    for slot, out_ref in enumerate(out_refs):
        invert(mixed.at[slot], back.at[slot], wide.at[slot], group, fast_inv, slow_inv, turn)
        collect(wide.at[slot], out_ref, group)


def add_kernel(*refs):
    total = refs[0][...].astype(F32)
    for one in refs[1:-1]:
        total = total + one[...].astype(F32)
    refs[-1][...] = total.astype(BF16)


def join_kernel(grad_ref, mine_ref, other_ref, out_ref):
    group = grad_ref.shape[1]
    out_ref[:, :group, :] = grad_ref[...]
    out_ref[:, group:, :] = (mine_ref[...].astype(F32) + other_ref[...].astype(F32)).astype(BF16)


def project_kernel(order_ref, conv_ref, query_ref, cot_ref, weight_ref, *out_refs):
    chans = query_ref.shape[1]
    gates = []
    for step in range(query_ref.shape[0] // LANES):
        rows = slice(step * LANES, (step + 1) * LANES)
        conv = flip(conv_ref[:, :, rows].reshape(-1, LANES))
        out_refs[4][rows, :] = times(cot_ref[rows, :], conv)
        gates.append(times(query_ref[rows, :], conv))
    for slot in range(4):
        columns = pl.ds(pl.multiple_of(order_ref[slot] * chans, chans), chans)
        for step, gate_out in enumerate(gates):
            rows = slice(step * LANES, (step + 1) * LANES)
            out_refs[slot][rows, :] = dot(gate_out, weight_ref[:, columns]).astype(BF16)


def finish_kernel(scale, in_ref, key_ref, value_ref, value_grad_ref, key_grad_ref, taps_grad_ref):
    group = in_ref.shape[1] // 2
    grad = flip(in_ref[:, :group, :].reshape(-1, in_ref.shape[-1]))
    value_grad_ref[...] = times(grad, key_ref[...])
    key_grad_ref[...] = times(grad, value_ref[...])
    terms = flip(in_ref[:, group:, :].reshape(-1, in_ref.shape[-1]))
    taps_grad_ref[...] = terms.astype(F32) * scale


VMEM = pl.BlockSpec(memory_space=pltpu.VMEM)
HBM = pl.BlockSpec(memory_space=pltpu.HBM)


def params(mebibytes=60):
    return pltpu.CompilerParams(vmem_limit_bytes=mebibytes * 1024 * 1024)


def cost(flops, moved):
    return pl.CostEstimate(flops=flops, bytes_accessed=moved, transcendentals=0)


def add_arrays(arrays, flops, name):
    return pl.pallas_call(
        add_kernel,
        in_specs=[VMEM] * len(arrays),
        out_specs=VMEM,
        out_shape=jax.ShapeDtypeStruct(arrays[0].shape, BF16),
        compiler_params=params(SMALL),
        cost_estimate=cost(flops, 2 * arrays[0].size * (len(arrays) + 1)),
        name=name,
    )(*arrays)


def shards(value_in, key_in, query_in, filter_taps, out_weight, cotangent):
    _, block, chans = value_in.shape
    sources = lax.axis_size("context")
    tensors = lax.axis_size("tensor")
    length = sources * block
    group = chans // sources
    radix = length // LANES
    value_in, key_in, query_in, cotangent = (
        one.reshape(block, chans) for one in (value_in, key_in, query_in, cotangent)
    )
    tables = right_angle_tables(sources, length)

    steps = chans // LANES
    sent = pl.pallas_call(
        gate_kernel,
        in_specs=[HBM] * 5,
        out_specs=VMEM,
        out_shape=jax.ShapeDtypeStruct((sources, 3 * group, block), BF16),
        scratch_shapes=[
            pltpu.VMEM((5, steps, block, LANES), BF16),
            pltpu.SemaphoreType.DMA((5, steps)),
        ],
        compiler_params=params(),
        cost_estimate=cost(6 * block * chans * LANES, 8 * 2 * block * chans),
        name="gate_and_turn",
    )(value_in, key_in, query_in, cotangent, filter_taps)
    received = lax.all_to_all(sent, "context", 0, 0, tiled=True)

    piece = jax.ShapeDtypeStruct((sources, group, block), BF16)
    rows = group * radix
    spectrum = (rows, 2 * LANES)
    wide = (block // LANES, sources * group, LANES)
    work = 6 * group * radix * LANES * 4 * LANES
    conv, terms, grad = pl.pallas_call(
        transform_kernel,
        in_specs=[VMEM] * 3,
        out_specs=[VMEM] * 3,
        out_shape=[piece] * 3,
        scratch_shapes=[
            pltpu.VMEM((3,) + wide, F32),
            pltpu.VMEM((3,) + spectrum, BF16),
            pltpu.VMEM((3,) + spectrum, F32),
            pltpu.VMEM((3,) + spectrum, BF16),
            pltpu.VMEM((3,) + spectrum, F32),
        ],
        compiler_params=params(MIDDLE),
        cost_estimate=cost(work, 8 * 2**20),
        name="transform",
    )(received, *tables)
    conv_back = lax.all_to_all(conv, "context", 0, 0, tiled=True)
    others = lax.ppermute(terms, "dp", [(0, 1), (1, 0)])

    at = lax.axis_index("tensor").astype(jnp.int32)
    last = tensors - 1
    mirrored = at > last - at

    def toward(chunk):
        return jnp.where(mirrored, last - chunk, chunk)

    outer = (at == 0) | (at == last)
    order = jnp.stack(
        [
            toward(3),
            toward(2),
            jnp.where(outer, toward(1), toward(0)),
            at,
        ]
    )
    steps = block // LANES
    square = jax.ShapeDtypeStruct((block, chans), BF16)
    slab = pl.BlockSpec((LANES, chans), lambda step: (step, 0))
    far, near, other, own, grad_query = pl.pallas_call(
        project_kernel,
        in_specs=[pl.BlockSpec(memory_space=pltpu.SMEM)] + [VMEM] * 4,
        out_specs=[VMEM] * 5,
        out_shape=[square] * 5,
        compiler_params=params(SMALL),
        cost_estimate=cost(2 * block * chans * chans * tensors, 6 * 2**20),
        name="project",
    )(order, conv_back, query_in, cotangent, out_weight)
    relayed = lax.ppermute(far, "tensor", [(0, 1), (3, 2)])
    across = lax.ppermute(near, "tensor", [(1, 2), (2, 1)])
    beyond = lax.ppermute(near, "tensor", [(0, 2), (3, 1)])
    beside = lax.ppermute(other, "tensor", [(0, 1), (3, 2), (1, 0), (2, 3)])
    both = add_arrays((far, relayed), 10**11, "relay")
    outward = lax.ppermute(both, "tensor", [(1, 3), (2, 0)])
    joined = pl.pallas_call(
        join_kernel,
        in_specs=[VMEM] * 3,
        out_specs=VMEM,
        out_shape=jax.ShapeDtypeStruct((sources, 2 * group, block), BF16),
        compiler_params=params(SMALL),
        cost_estimate=cost(2 * 10**9, 5 * 2 * block * chans),
        name="join",
    )(grad, terms, others)
    mixed_out = add_arrays(
        (own, across, beyond, beside, outward), 10**11, "add_parts"
    )
    grads_back = lax.all_to_all(joined, "context", 0, 0, tiled=True)
    scale = 1.0 / math.sqrt(lax.axis_size("dp") * length)
    grad_value, grad_key, grad_filter = pl.pallas_call(
        functools.partial(finish_kernel, scale),
        grid=(steps,),
        in_specs=[
            pl.BlockSpec((sources, 2 * group, LANES), lambda step: (0, 0, step)),
            slab,
            slab,
        ],
        out_specs=[slab] * 3,
        out_shape=[
            jax.ShapeDtypeStruct((block, chans), BF16),
            jax.ShapeDtypeStruct((block, chans), BF16),
            jax.ShapeDtypeStruct((block, chans), F32),
        ],
        compiler_params=params(SMALL),
        cost_estimate=cost(4 * block * chans * LANES, 10 * block * chans),
        name="finish",
    )(grads_back, key_in, value_in)
    return (
        mixed_out[None],
        grad_value[None],
        grad_key[None],
        grad_query[None],
        grad_filter,
    )


def solution(mesh):
    whole = P("dp", "context", "tensor")
    return jax.shard_map(
        shards,
        mesh=mesh,
        in_specs=(whole, whole, whole, P("context", "tensor"), P("tensor", None), whole),
        out_specs=(whole, whole, whole, whole, P("context", "tensor")),
        check_vma=False,
    )
```

```python
import functools
import math

import jax
import jax.numpy as jnp
import numpy as np
from jax import lax
from jax.experimental import pallas as pl
from jax.experimental.pallas import tpu as pltpu
from jax.sharding import PartitionSpec as P

LANES = 128
F32 = jnp.float32
BF16 = jnp.bfloat16
SMALL = 16
MIDDLE = 36
ADD = 60
PROJECT = 60


def right_angle_tables(source_count, length):
    radix = length // LANES
    quarters = radix // source_count
    row = np.arange(radix)
    slow = (row % source_count) * quarters + row // source_count
    freq = np.arange(radix) + 0.25
    slow_angle = -2.0 * np.pi * freq[:, None] * slow[None, :] / radix
    slow_fwd = np.concatenate([np.cos(slow_angle), np.sin(slow_angle)], 0)
    slow_inv = slow_fwd.T
    fast = np.arange(LANES)
    turn_angle = -2.0 * np.pi * freq[:, None] * fast[None, :] / length
    turn_cos, turn_sin = np.cos(turn_angle), np.sin(turn_angle)
    fast_angle = -2.0 * np.pi * ((fast[:, None] * fast[None, :]) % LANES) / LANES
    fast_cos, fast_sin = np.cos(fast_angle), np.sin(fast_angle)
    fast_fwd = np.block([[fast_cos, fast_sin], [-fast_sin, fast_cos]])
    fast_inv = np.block([[fast_cos, -fast_sin], [fast_sin, fast_cos]])
    turn = np.stack([turn_cos, turn_sin, turn_cos / length, turn_sin / length])
    slow_fwd = np.concatenate([slow_fwd, np.zeros_like(slow_fwd)], 1)
    factors = np.concatenate([slow_fwd, fast_fwd, fast_inv, slow_inv], 0)
    return (jnp.asarray(factors, BF16), jnp.asarray(turn, F32))


def factors_of(factors_ref):
    size = 2 * LANES
    return (
        factors_ref.at[:size, :LANES],
        factors_ref.at[size : 2 * size, :],
        factors_ref.at[2 * size : 3 * size, :],
        factors_ref.at[3 * size :, :],
    )


def dot(left, right):
    return jnp.dot(left, right, preferred_element_type=F32)


def flip(square):
    extent = square.shape[1]
    rows = lax.broadcasted_iota(jnp.int32, (extent, extent), 0)
    cols = lax.broadcasted_iota(jnp.int32, (extent, extent), 1)
    unit = jnp.where(rows == cols, 1.0, 0.0).astype(BF16)
    turned = lax.dot_general(unit, square, (((1,), (1,)), ((), ())), preferred_element_type=F32)
    return turned.astype(BF16)


def times(left, right):
    return (left.astype(F32) * right.astype(F32)).astype(BF16)


def gate_kernel(*refs):
    in_refs, (out_hbm, held, out_ref, arrival, departure) = refs[:5], refs[5:]
    _, chunks, _, width = held.shape

    def copy(one, chunk):
        return pltpu.make_async_copy(
            in_refs[one].at[:, pl.ds(chunk * width, width)],
            held.at[one, chunk],
            arrival.at[one, chunk],
        )

    for chunk in range(chunks):
        for one in range(5):
            copy(one, chunk).start()
    group = out_ref.shape[1] // 3
    share = out_ref.shape[0] // chunks

    def send(chunk):
        part = pl.ds(chunk * share, share)
        return pltpu.make_async_copy(out_ref.at[part], out_hbm.at[part], departure.at[chunk])

    for chunk in range(chunks):
        for one in range(5):
            copy(one, chunk).wait()
        value, key, query, cotangent, taps = (held[one, chunk] for one in range(5))
        for slot, signal in enumerate((times(key, value), taps, times(cotangent, query))):
            turned = flip(signal)
            out_ref[
                chunk * share : (chunk + 1) * share, slot * group : (slot + 1) * group, :
            ] = turned.reshape(share, group, turned.shape[1])
        send(chunk).start()
    for chunk in range(chunks):
        send(chunk).wait()


def spread(in_ref, first_row, wide_ref, group):
    for source in range(in_ref.shape[0]):
        rows = in_ref[source, first_row : first_row + group, :].astype(F32)
        for quarter in range(wide_ref.shape[0]):
            wide_ref[quarter, source * group : (source + 1) * group, :] = rows[
                :, quarter * LANES : (quarter + 1) * LANES
            ]


def turn_forward(wide_ref, turned_ref, group, slow_fwd, turn):
    quarters, rows, _ = wide_ref.shape
    turn_cos, turn_sin = turn[0], turn[1]
    for chan in range(0, group, 2):
        columns = [
            jnp.concatenate(
                [wide_ref[q, pl.ds(one, rows // group, stride=group), :] for q in range(quarters)],
                0,
            )
            for one in (chan, chan + 1)
        ]
        first = dot(slow_fwd[...], jnp.concatenate(columns, 1).astype(BF16))
        radix = first.shape[0] // 2
        for side in range(2):
            lanes = slice(side * LANES, (side + 1) * LANES)
            part_re, part_im = first[:radix, lanes], first[radix:, lanes]
            out_rows = slice((chan + side) * radix, (chan + side + 1) * radix)
            turned_ref[out_rows, :LANES] = (part_re * turn_cos - part_im * turn_sin).astype(BF16)
            turned_ref[out_rows, LANES:] = (part_re * turn_sin + part_im * turn_cos).astype(BF16)


def product(left, right, conjugate):
    left_re, left_im = left[:, :LANES], left[:, LANES:]
    right_re, right_im = right[:, :LANES], right[:, LANES:]
    if conjugate:
        both_re = left_re * right_re + left_im * right_im
        both_im = left_re * right_im - left_im * right_re
    else:
        both_re = left_re * right_re - left_im * right_im
        both_im = left_re * right_im + left_im * right_re
    return jnp.concatenate([both_re, both_im], 1).astype(BF16)


def invert(spectrum_ref, back_ref, wide_ref, group, fast_inv, slow_inv, turn):
    back_ref[...] = dot(spectrum_ref[...], fast_inv[...])
    quarters, rows, _ = wide_ref.shape
    sources = rows // group
    radix = back_ref.shape[0] // group
    turn_cos, turn_sin = turn[2], turn[3]
    for chan in range(0, group, 2):
        parts_re, parts_im = [], []
        for one in (chan, chan + 1):
            in_rows = slice(one * radix, (one + 1) * radix)
            back_re, back_im = back_ref[in_rows, :LANES], back_ref[in_rows, LANES:]
            parts_re.append((back_re * turn_cos + back_im * turn_sin).astype(BF16))
            parts_im.append((back_im * turn_cos - back_re * turn_sin).astype(BF16))
        unturned = jnp.concatenate(
            [jnp.concatenate(parts_re, 1), jnp.concatenate(parts_im, 1)], 0
        )
        signal = dot(slow_inv[...], unturned)
        for side in range(2):
            one = signal[:, side * LANES : (side + 1) * LANES]
            for q in range(quarters):
                wide_ref[q, pl.ds(chan + side, sources, stride=group), :] = one[
                    q * sources : (q + 1) * sources
                ]


def collect(wide_ref, out_ref, group):
    for source in range(out_ref.shape[0]):
        out_ref[source, :group, :] = jnp.concatenate(
            [
                wide_ref[quarter, source * group : (source + 1) * group, :]
                for quarter in range(wide_ref.shape[0])
            ],
            1,
        ).astype(BF16)


def transform_kernel(in_ref, factors_ref, turn, *refs):
    slow_fwd, fast_fwd, fast_inv, slow_inv = factors_of(factors_ref)
    out_refs, (wide, turned, spectra, mixed, back) = refs[:3], refs[3:]
    group = out_refs[0].shape[1]
    for slot in range(3):
        spread(in_ref, slot * group, wide.at[slot], group)
        turn_forward(wide.at[slot], turned.at[slot], group, slow_fwd, turn)
        spectra[slot] = dot(turned[slot], fast_fwd[...])
    rows = spectra.shape[1] // group
    for chan in range(group):
        part = slice(chan * rows, (chan + 1) * rows)
        gated, taps, dconv = (spectra[slot, part, :] for slot in range(3))
        mixed[0, part, :] = product(gated, taps, False)
        mixed[1, part, :] = product(gated, dconv, True)
        mixed[2, part, :] = product(taps, dconv, True)
    for slot, out_ref in enumerate(out_refs):
        invert(mixed.at[slot], back.at[slot], wide.at[slot], group, fast_inv, slow_inv, turn)
        collect(wide.at[slot], out_ref, group)


def add_kernel(*refs):
    total = refs[0][...].astype(F32)
    for one in refs[1:-1]:
        total = total + one[...].astype(F32)
    refs[-1][...] = total.astype(BF16)


def join_kernel(grad_ref, mine_ref, other_ref, out_ref):
    group = grad_ref.shape[1]
    out_ref[:, :group, :] = grad_ref[...]
    out_ref[:, group:, :] = (mine_ref[...].astype(F32) + other_ref[...].astype(F32)).astype(BF16)


def project_kernel(order_ref, conv_ref, query_ref, cot_ref, weight_ref, *out_refs):
    chans = query_ref.shape[1]
    gates = []
    for step in range(query_ref.shape[0] // LANES):
        rows = slice(step * LANES, (step + 1) * LANES)
        conv = flip(conv_ref[:, :, rows].reshape(-1, LANES))
        out_refs[4][rows, :] = times(cot_ref[rows, :], conv)
        gates.append(times(query_ref[rows, :], conv))
    for slot in range(4):
        columns = pl.ds(pl.multiple_of(order_ref[slot] * chans, chans), chans)
        for step, gate_out in enumerate(gates):
            rows = slice(step * LANES, (step + 1) * LANES)
            out_refs[slot][rows, :] = dot(gate_out, weight_ref[:, columns]).astype(BF16)


def finish_kernel(scale, in_ref, key_ref, value_ref, value_grad_ref, key_grad_ref, taps_grad_ref):
    group = in_ref.shape[1] // 2
    grad = flip(in_ref[:, :group, :].reshape(-1, in_ref.shape[-1]))
    value_grad_ref[...] = times(grad, key_ref[...])
    key_grad_ref[...] = times(grad, value_ref[...])
    terms = flip(in_ref[:, group:, :].reshape(-1, in_ref.shape[-1]))
    taps_grad_ref[...] = terms.astype(F32) * scale


VMEM = pl.BlockSpec(memory_space=pltpu.VMEM)
HBM = pl.BlockSpec(memory_space=pltpu.HBM)


def params(mebibytes=60):
    return pltpu.CompilerParams(vmem_limit_bytes=mebibytes * 1024 * 1024)


def cost(flops, moved):
    return pl.CostEstimate(flops=flops, bytes_accessed=moved, transcendentals=0)


def add_arrays(arrays, flops, name):
    return pl.pallas_call(
        add_kernel,
        in_specs=[VMEM] * len(arrays),
        out_specs=VMEM,
        out_shape=jax.ShapeDtypeStruct(arrays[0].shape, BF16),
        compiler_params=params(SMALL),
        cost_estimate=cost(flops, 2 * arrays[0].size * (len(arrays) + 1)),
        name=name,
    )(*arrays)


def shards(value_in, key_in, query_in, filter_taps, out_weight, cotangent):
    _, block, chans = value_in.shape
    sources = lax.axis_size("context")
    tensors = lax.axis_size("tensor")
    length = sources * block
    group = chans // sources
    radix = length // LANES
    value_in, key_in, query_in, cotangent = (
        one.reshape(block, chans) for one in (value_in, key_in, query_in, cotangent)
    )
    tables = right_angle_tables(sources, length)

    steps = chans // LANES
    sent = pl.pallas_call(
        gate_kernel,
        in_specs=[HBM] * 5,
        out_specs=HBM,
        out_shape=jax.ShapeDtypeStruct((sources, 3 * group, block), BF16),
        scratch_shapes=[
            pltpu.VMEM((5, steps, block, LANES), BF16),
            pltpu.VMEM((sources, 3 * group, block), BF16),
            pltpu.SemaphoreType.DMA((5, steps)),
            pltpu.SemaphoreType.DMA((steps,)),
        ],
        compiler_params=params(),
        cost_estimate=cost(6 * block * chans * LANES, 8 * 2 * block * chans),
        name="gate_and_turn",
    )(value_in, key_in, query_in, cotangent, filter_taps)
    received = lax.all_to_all(sent, "context", 0, 0, tiled=True)

    piece = jax.ShapeDtypeStruct((sources, group, block), BF16)
    rows = group * radix
    spectrum = (rows, 2 * LANES)
    wide = (block // LANES, sources * group, LANES)
    work = 6 * group * radix * LANES * 4 * LANES
    conv, terms, grad = pl.pallas_call(
        transform_kernel,
        in_specs=[VMEM] * 3,
        out_specs=[VMEM] * 3,
        out_shape=[piece] * 3,
        scratch_shapes=[
            pltpu.VMEM((3,) + wide, F32),
            pltpu.VMEM((3,) + spectrum, BF16),
            pltpu.VMEM((3,) + spectrum, F32),
            pltpu.VMEM((3,) + spectrum, BF16),
            pltpu.VMEM((3,) + spectrum, F32),
        ],
        compiler_params=params(MIDDLE),
        cost_estimate=cost(work, 8 * 2**20),
        name="transform",
    )(received, *tables)
    conv_back = lax.all_to_all(conv, "context", 0, 0, tiled=True)
    others = lax.ppermute(terms, "dp", [(0, 1), (1, 0)])

    at = lax.axis_index("tensor").astype(jnp.int32)
    last = tensors - 1
    mirrored = at > last - at

    def toward(chunk):
        return jnp.where(mirrored, last - chunk, chunk)

    outer = (at == 0) | (at == last)
    order = jnp.stack(
        [
            toward(3),
            toward(2),
            jnp.where(outer, toward(1), toward(0)),
            at,
        ]
    )
    steps = block // LANES
    square = jax.ShapeDtypeStruct((block, chans), BF16)
    slab = pl.BlockSpec((LANES, chans), lambda step: (step, 0))
    far, near, other, own, grad_query = pl.pallas_call(
        project_kernel,
        in_specs=[pl.BlockSpec(memory_space=pltpu.SMEM)] + [VMEM] * 4,
        out_specs=[VMEM] * 5,
        out_shape=[square] * 5,
        compiler_params=params(SMALL),
        cost_estimate=cost(2 * block * chans * chans * tensors, 6 * 2**20),
        name="project",
    )(order, conv_back, query_in, cotangent, out_weight)
    relayed = lax.ppermute(far, "tensor", [(0, 1), (3, 2)])
    across = lax.ppermute(near, "tensor", [(1, 2), (2, 1)])
    beyond = lax.ppermute(near, "tensor", [(0, 2), (3, 1)])
    beside = lax.ppermute(other, "tensor", [(0, 1), (3, 2), (1, 0), (2, 3)])
    both = add_arrays((far, relayed), 10**11, "relay")
    outward = lax.ppermute(both, "tensor", [(1, 3), (2, 0)])
    joined = pl.pallas_call(
        join_kernel,
        in_specs=[VMEM] * 3,
        out_specs=VMEM,
        out_shape=jax.ShapeDtypeStruct((sources, 2 * group, block), BF16),
        compiler_params=params(SMALL),
        cost_estimate=cost(2 * 10**9, 5 * 2 * block * chans),
        name="join",
    )(grad, terms, others)
    mixed_out = add_arrays(
        (own, across, beyond, beside, outward), 10**11, "add_parts"
    )
    grads_back = lax.all_to_all(joined, "context", 0, 0, tiled=True)
    scale = 1.0 / math.sqrt(lax.axis_size("dp") * length)
    grad_value, grad_key, grad_filter = pl.pallas_call(
        functools.partial(finish_kernel, scale),
        grid=(steps,),
        in_specs=[
            pl.BlockSpec((sources, 2 * group, LANES), lambda step: (0, 0, step)),
            slab,
            slab,
        ],
        out_specs=[slab] * 3,
        out_shape=[
            jax.ShapeDtypeStruct((block, chans), BF16),
            jax.ShapeDtypeStruct((block, chans), BF16),
            jax.ShapeDtypeStruct((block, chans), F32),
        ],
        compiler_params=params(SMALL),
        cost_estimate=cost(4 * block * chans * LANES, 10 * block * chans),
        name="finish",
    )(grads_back, key_in, value_in)
    return (
        mixed_out[None],
        grad_value[None],
        grad_key[None],
        grad_query[None],
        grad_filter,
    )


def solution(mesh):
    whole = P("dp", "context", "tensor")
    return jax.shard_map(
        shards,
        mesh=mesh,
        in_specs=(whole, whole, whole, P("context", "tensor"), P("tensor", None), whole),
        out_specs=(whole, whole, whole, whole, P("context", "tensor")),
        check_vma=False,
    )
```
